512 devices in a mesh: segment: 8 (over y, core), seq: 16 (over x, z_hi), tp: 4 (over z_lo).
Axes of the slice: x: 4, y: 4, z: 16 (z_hi: 4, z_lo: 4; z = z_hi * 4 + z_lo), core: 2. Of those that a mesh axis runs over, the one named last changes fastest.
Arguments:
- queries: bfloat16 [8, 3072, 4096], P('segment', 'seq', 'tp'), may hold values from -64 to 64
- nb_keys: bfloat16 [8, 48, 256, 4096], P('segment', 'seq', None, 'tp'), may hold values from -24 to 24
- nb_values: bfloat16 [8, 48, 256, 4096], P('segment', 'seq', None, 'tp'), may hold values from -6 to 6
- nb_lengths: int32 [8, 48, 2], P('segment', 'seq'), may hold values from 1 to 128
- slot_stretch: int32 [8, 48], P('segment', 'seq'), may hold values from 0 to 47, as said below
- out_weight: bfloat16 [8, 4096, 4096], P('segment', 'tp', 'seq'), may hold values from -0.09375 to 0.09375
- residual: bfloat16 [8, 3072, 4096], P('segment', 'seq', 'tp'), may hold values from -6 to 6
Outputs:
- mixed: bfloat16 [8, 3072, 4096], P('segment', 'seq', 'tp')
The draws below stay inside these ranges and needn't reach their ends.
Inputs may be any that keep to these rules, and one draw needn't show every extreme that they name: Each row slot_stretch[e] is a permutation of the 48 stretches. The 3 stretches of one decoder device (stretches i * 3 to i * 3 + 2) are served by slots on 3 different encoder devices, so one decoder device sends at most one stretch to one encoder device.
All inputs are finite; a program needn't handle non-finite values.
Results may differ from the reference program's by a relative error of at most 0.0034.
Values may be sent and summed in bfloat16 or wider, within the bound.
No kernel may reach another device: no remote copies, remote signals or barrier semaphores. Data moves between devices by JAX's collectives and lax.ppermute only.
A program may use at most 64 MiB of HBM per device.

```python
import math
import jax
import jax.numpy as jnp
from jax import lax

D = 4096
HEADS = 32
HD = 128
STRETCH = 64
NR = 128
KN = 2
CH_DEV = 3
HA = 4096
NCHUNK = 48
TOKENS = 3072
N_SEGMENT = 8
N_SEQ = 16


def draw_queries(key, part):
    key = jax.random.fold_in(key, 5)
    first = jax.random.fold_in(key, 0)
    base = jax.random.normal(first, (N_SEGMENT, TOKENS, HEADS, HD), jnp.float32)
    return jnp.clip(base, -64.0, 64.0).reshape(N_SEGMENT, TOKENS, HEADS * HD).astype(jnp.bfloat16)


def draw_nb_keys(key, part):
    key = jax.random.fold_in(key, 7)
    first = jax.random.fold_in(key, 0)
    base = jax.random.normal(first, (N_SEGMENT, NCHUNK, KN * NR, HEADS, HD), jnp.float32)
    return jnp.clip(base, -24.0, 24.0).reshape(N_SEGMENT, NCHUNK, KN * NR, HEADS * HD).astype(jnp.bfloat16)


def draw_slot_stretch(key, part):
    key = jax.random.fold_in(key, 9)

    def one_section(section_key):
        key_a, key_b, key_c, key_d = jax.random.split(section_key, 4)
        spread = jax.random.permutation(key_a, N_SEQ)
        order = jax.random.permutation(key_b, N_SEQ)
        offsets = jax.random.permutation(key_c, N_SEQ)[:CH_DEV]
        places = jax.random.permutation(key_d, CH_DEV)
        owners = jnp.arange(N_SEQ, dtype=jnp.int32)[:, None]
        within = jnp.arange(CH_DEV, dtype=jnp.int32)[None, :]
        holders = spread[(order[owners] + offsets[within]) % N_SEQ]
        slots = holders * CH_DEV + places[within]
        stretches = owners * CH_DEV + within
        return jnp.zeros((NCHUNK,), jnp.int32).at[slots.reshape(-1)].set(stretches.reshape(-1))
    return jax.vmap(one_section)(jax.random.split(key, N_SEGMENT))


def plant(values, stream_key, least, largest):
    extent = values.shape
    place = [jax.random.randint(jax.random.fold_in(stream_key, axis), (), 0, extent[axis]) for axis in range(len(extent))]
    values = values.at[tuple(place)].set(least)
    longest = extent.index(max(extent))
    place[longest] = (place[longest] + 1) % extent[longest]
    return values.at[tuple(place)].set(largest)


def block_scale(own_key, dims, cuts, low, largest):
    gain = 1.0
    for dim, blocks in cuts:
        draws = jax.random.uniform(jax.random.fold_in(jax.random.fold_in(own_key, 6), dim), (blocks,), jnp.float32, low / len(cuts), largest / len(cuts))
        gain = gain * jnp.repeat(jnp.exp(draws), dims[dim] // blocks).reshape((-1,) + (1,) * (len(dims) - 1 - dim))
    return gain


def bell_draw(stream_key, shape, scale, limit, shards=(), held_as=jnp.bfloat16):
    array = scale * jax.random.normal(stream_key, shape, jnp.float32)
    if shards:
        array = array * block_scale(stream_key, shape, shards, -0.22, 0.18)
    return jnp.clip(array, -limit, limit).astype(held_as)


def setup_inputs(seed: int = 0) -> dict:
    seeds = jax.random.split(jax.random.key(seed), 8)
    return {
        "queries": draw_queries(jax.random.fold_in(seeds[7], 71), 0),
        "nb_keys": draw_nb_keys(jax.random.fold_in(seeds[7], 71), 0),
        "nb_values": bell_draw(seeds[2], (N_SEGMENT, NCHUNK, KN * NR, HA), 1.0, 6.0, ((0, 8), (1, 16), (3, 4))),
        "nb_lengths": plant(jax.random.randint(seeds[3], (N_SEGMENT, NCHUNK, KN), 1, NR + 1), jax.random.fold_in(seeds[3], 1), 1, NR).astype(jnp.int32),
        "slot_stretch": draw_slot_stretch(jax.random.fold_in(seeds[7], 71), 0),
        "out_weight": bell_draw(seeds[5], (N_SEGMENT, HA, D), HA ** -0.5, 0.09375, ((0, 8), (1, 4), (2, 16))),
        "residual": bell_draw(seeds[6], (N_SEGMENT, TOKENS, D), 1.0, 6.0, ((0, 8), (1, 16), (2, 4))),
    }


def attend(query_rows, key_rows, value_rows, lengths):
    count, width, feats = query_rows.shape
    span = key_rows.shape[1]
    query_heads = query_rows.reshape(count, width, HEADS, HD).astype(jnp.float32)
    key_heads = key_rows.reshape(count, span, HEADS, HD).astype(jnp.float32)
    value_heads = value_rows.reshape(count, span, HEADS, HD).astype(jnp.float32)
    scores = jnp.einsum('cqhd,clhd->chql', query_heads, key_heads) * (1.0 / math.sqrt(HD))
    position = jnp.arange(span, dtype=jnp.int32)
    limits = jnp.take(lengths, position // NR, axis=1)
    valid = ((position % NR)[None, :] < limits)[:, None, None, :]
    highest = lax.optimization_barrier(jnp.max(jnp.where(valid, scores, -1e+30), axis=-1, keepdims=True))
    expo = jnp.exp(jnp.where(valid, scores - highest, -1e+30))
    weights = (expo / lax.optimization_barrier(jnp.sum(expo, axis=-1, keepdims=True))).astype(jnp.bfloat16)
    mixed = jnp.einsum('chql,clhd->cqhd', weights.astype(jnp.float32), value_heads)
    return mixed.astype(jnp.bfloat16).reshape(count * width, feats)

def reference(queries, nb_keys, nb_values, nb_lengths, slot_stretch, out_weight, residual):
    results = []
    for section in range(N_SEGMENT):
        source = (section - 1) % N_SEGMENT
        inverse = jnp.zeros((NCHUNK,), jnp.int32).at[slot_stretch[source]].set(jnp.arange(NCHUNK, dtype=jnp.int32))
        key_rows = jnp.take(nb_keys[source], inverse, axis=0)
        value_rows = jnp.take(nb_values[source], inverse, axis=0)
        lengths = jnp.take(nb_lengths[source], inverse, axis=0)
        query_rows = queries[section].reshape(NCHUNK, STRETCH, HEADS * HD)
        cca = attend(query_rows, key_rows, value_rows, lengths)
        projected = jnp.dot(cca, out_weight[section], preferred_element_type=jnp.float32)
        results.append((residual[section].astype(jnp.float32) + projected).astype(jnp.bfloat16))
    return jnp.stack(results)
```

```python
import functools
import math

import jax
import jax.numpy as jnp
from jax import lax
from jax.experimental import pallas as pl
from jax.experimental.pallas import tpu as pltpu
from jax.sharding import Mesh
from jax.sharding import PartitionSpec as P

HD = 128
STRETCH = 64
NR = 128
G = 4
ROWS = STRETCH // G
VMEM = pl.BlockSpec(memory_space=pltpu.VMEM)
SMEM = pl.BlockSpec(memory_space=pltpu.SMEM)
PARAMS = pltpu.CompilerParams(vmem_limit_bytes=40 * 1024 * 1024)
SEQ = ("x", "zh")


def cost(flops, moved, trans=0):
    return pl.CostEstimate(flops=flops, bytes_accessed=moved, transcendentals=trans)


def permute_kernel(order_ref, in_ref, out_ref):
    for slot in range(in_ref.shape[0]):
        out_ref[slot] = in_ref[order_ref[slot]]


def permute_blocks(blocks, order):
    return pl.pallas_call(
        permute_kernel,
        out_shape=jax.ShapeDtypeStruct(blocks.shape, blocks.dtype),
        in_specs=[SMEM, VMEM],
        out_specs=VMEM,
        compiler_params=PARAMS,
        cost_estimate=cost(0, 4 * blocks.size),
        name="permute_blocks",
    )(order, blocks)


def attend_kernel(len_ref, q_ref, k_ref, v_ref, out_ref):
    slot = pl.program_id(0)
    span = k_ref.shape[1]
    heads = k_ref.shape[2] // HD
    per_group = heads // G
    position = lax.broadcasted_iota(jnp.int32, (1, span), 1)
    limit = jnp.where(position < NR, len_ref[slot, 0], len_ref[slot, 1] + NR)
    valid = position < limit
    for head in range(heads):
        lanes = slice(head * HD, (head + 1) * HD)
        part = slice((head % per_group) * HD, (head % per_group + 1) * HD)
        q = q_ref[:, head // per_group, 0, :, part].reshape(STRETCH, HD)
        scores = lax.dot_general(
            q, k_ref[0, :, lanes], (((1,), (1,)), ((), ())), preferred_element_type=jnp.float32
        ) * (1.0 / math.sqrt(HD))
        highest = jnp.max(jnp.where(valid, scores, -1e30), axis=-1, keepdims=True)
        expo = jnp.exp(jnp.where(valid, scores - highest, -1e30))
        weights = (expo / jnp.sum(expo, axis=-1, keepdims=True)).astype(jnp.bfloat16)
        mixed = jnp.dot(weights, v_ref[0, :, lanes], preferred_element_type=jnp.float32)
        out_ref[:, 0, :, lanes] = mixed.astype(jnp.bfloat16).reshape(G, ROWS, HD)


def attend(picked, keys, values, lengths):
    slots, span, feats = keys.shape
    return pl.pallas_call(
        attend_kernel,
        out_shape=jax.ShapeDtypeStruct((G, slots, ROWS, feats), jnp.bfloat16),
        grid=(slots,),
        in_specs=[
            SMEM,
            pl.BlockSpec((G, G, 1, ROWS, feats // G), lambda s: (0, 0, s, 0, 0)),
            pl.BlockSpec((1, span, feats), lambda s: (s, 0, 0)),
            pl.BlockSpec((1, span, feats), lambda s: (s, 0, 0)),
        ],
        out_specs=pl.BlockSpec((G, 1, ROWS, feats), lambda s: (0, s, 0, 0)),
        compiler_params=PARAMS,
        cost_estimate=cost(4 * slots * STRETCH * span * feats, 4 * slots * span * feats),
        name="attend",
    )(lengths, picked, keys, values)


def project_kernel(a_ref, w_ref, out_ref):
    out_ref[0] = jnp.dot(a_ref[...], w_ref[...], preferred_element_type=jnp.float32).astype(
        jnp.bfloat16
    )


def project(rows, weight):
    m, k = rows.shape
    n = weight.shape[1]
    return pl.pallas_call(
        project_kernel,
        out_shape=jax.ShapeDtypeStruct((G, m, n // G), jnp.bfloat16),
        grid=(G,),
        in_specs=[
            pl.BlockSpec((m, k), lambda c: (0, 0)),
            pl.BlockSpec((k, n // G), lambda c: (0, c)),
        ],
        out_specs=pl.BlockSpec((1, m, n // G), lambda c: (c, 0, 0)),
        compiler_params=PARAMS,
        cost_estimate=cost(2 * m * n * k, 2 * (m * k + n * k + m * n)),
        name="project",
    )(rows, weight)


def sum_permute_kernel(order_ref, in_ref, out_ref):
    for place in range(out_ref.shape[0]):
        taken = order_ref[place]
        total = in_ref[0, taken].astype(jnp.float32)
        for part in range(1, in_ref.shape[0]):
            total = total + in_ref[part, taken].astype(jnp.float32)
        out_ref[place] = total.astype(out_ref.dtype)


def sum_permute(parts, order):
    return pl.pallas_call(
        sum_permute_kernel,
        out_shape=jax.ShapeDtypeStruct(parts.shape[1:], parts.dtype),
        in_specs=[SMEM, VMEM],
        out_specs=VMEM,
        compiler_params=PARAMS,
        cost_estimate=cost(parts.size, 3 * parts.size),
        name="sum_permute",
    )(order, parts)


def exchange(value, axes):
    return lax.all_to_all(value, axes, split_axis=0, concat_axis=0, tiled=True)


def local(queries, nb_keys, nb_values, nb_lengths, slot_stretch, out_weight, residual):
    per_dev = slot_stretch.shape[1]
    feats = queries.shape[2]
    part = feats // G
    sections = lax.axis_size("segment")
    count = per_dev * G * G
    back = [(i, (i - 1) % sections) for i in range(sections)]

    weight = lax.ppermute(out_weight[0], "segment", back)
    weight = lax.all_gather(weight, "zh", axis=1, tiled=True)

    table = lax.all_gather(slot_stretch[0], SEQ, axis=0, tiled=True)
    ids = jnp.arange(count, dtype=jnp.int32)
    inverse = jnp.sum(jnp.where(table[None, :] == ids[:, None], ids[None, :], 0), axis=1)

    pieces = queries[0].reshape(per_dev, G, ROWS, G, part).transpose(1, 3, 0, 2, 4)
    pieces = lax.ppermute(pieces, "segment", back)
    spread = exchange(pieces.reshape(G * G, per_dev, ROWS, part), SEQ)
    ordered = permute_blocks(spread.reshape(count, ROWS, part), table)
    picked = exchange(ordered.reshape(G * G, per_dev, ROWS, part), SEQ)

    answer = attend(
        picked.reshape(G, G, per_dev, ROWS, part), nb_keys[0], nb_values[0], nb_lengths[0]
    )
    banded = exchange(answer, "zh")
    everywhere = jnp.broadcast_to(banded[None], (G,) + banded.shape)
    gathered = exchange(everywhere, "x")

    partial = project(gathered.reshape(count * ROWS, feats), weight)
    partial = exchange(partial, "tp").reshape(G, count, ROWS, part)
    summed = sum_permute(partial, inverse)

    moves = []
    for s in range(sections):
        for x in range(G):
            for zh in range(G):
                for t in range(G):
                    source = ((s * G + x) * G + zh) * G + t
                    target = ((((s + 1) % sections) * G + t) * G + zh) * G + x
                    moves.append((source, target))
    turned = lax.ppermute(summed, ("segment", "x", "zh", "tp"), moves)
    owned = exchange(turned.reshape(G * G, per_dev, ROWS, part), SEQ)
    owned = owned.reshape(G, G, per_dev, ROWS, part).transpose(2, 1, 3, 0, 4)
    projected = owned.reshape(per_dev * STRETCH, feats).astype(jnp.float32)
    return (residual[0].astype(jnp.float32) + projected).astype(jnp.bfloat16)[None]


def solution(mesh):
    sections, _, tp = mesh.devices.shape
    inner = Mesh(mesh.devices.reshape(sections, G, G, tp), ("segment", "x", "zh", "tp"))
    in_specs = (
        P("segment", SEQ, "tp"),
        P("segment", SEQ, None, "tp"),
        P("segment", SEQ, None, "tp"),
        P("segment", SEQ, None),
        P("segment", SEQ),
        P("segment", "tp", SEQ),
        P("segment", SEQ, "tp"),
    )
    out_specs = P("segment", SEQ, "tp")
    return jax.shard_map(local, mesh=inner, in_specs=in_specs, out_specs=out_specs, check_vma=False)
```

```python
import functools
import math

import jax
import jax.numpy as jnp
from jax import lax
from jax.experimental import pallas as pl
from jax.experimental.pallas import tpu as pltpu
from jax.sharding import Mesh
from jax.sharding import PartitionSpec as P

HD = 128
STRETCH = 64
NR = 128
G = 4
ROWS = STRETCH // G
VMEM = pl.BlockSpec(memory_space=pltpu.VMEM)
SMEM = pl.BlockSpec(memory_space=pltpu.SMEM)
PARAMS = pltpu.CompilerParams(vmem_limit_bytes=40 * 1024 * 1024)
SEQ = ("x", "zh")


def cost(flops, moved, trans=0):
    return pl.CostEstimate(flops=flops, bytes_accessed=moved, transcendentals=trans)


def permute_kernel(per_dev, order_ref, in_ref, out_ref):
    for slot in range(out_ref.shape[0]):
        taken = order_ref[slot]
        start = pl.multiple_of(lax.rem(taken, per_dev) * ROWS, ROWS)
        out_ref[slot] = in_ref[lax.div(taken, per_dev), pl.ds(start, ROWS), :]


def permute_blocks(spread, order, per_dev):
    sources, _, part = spread.shape
    return pl.pallas_call(
        functools.partial(permute_kernel, per_dev),
        out_shape=jax.ShapeDtypeStruct((sources * per_dev, ROWS, part), spread.dtype),
        in_specs=[SMEM, VMEM],
        out_specs=VMEM,
        compiler_params=PARAMS,
        cost_estimate=cost(0, 4 * spread.size),
        name="permute_blocks",
    )(order, spread)


def attend_kernel(len_ref, q_ref, k_ref, v_ref, out_ref):
    slot = pl.program_id(0)
    span = k_ref.shape[1]
    heads = k_ref.shape[2] // HD
    per_group = heads // G
    position = lax.broadcasted_iota(jnp.int32, (1, span), 1)
    limit = jnp.where(position < NR, len_ref[slot, 0], len_ref[slot, 1] + NR)
    valid = position < limit
    for head in range(heads):
        lanes = slice(head * HD, (head + 1) * HD)
        part = slice((head % per_group) * HD, (head % per_group + 1) * HD)
        q = q_ref[:, head // per_group, 0, :, part].reshape(STRETCH, HD)
        scores = lax.dot_general(
            q, k_ref[0, :, lanes], (((1,), (1,)), ((), ())), preferred_element_type=jnp.float32
        ) * (1.0 / math.sqrt(HD))
        highest = jnp.max(jnp.where(valid, scores, -1e30), axis=-1, keepdims=True)
        expo = jnp.exp(jnp.where(valid, scores - highest, -1e30))
        weights = (expo / jnp.sum(expo, axis=-1, keepdims=True)).astype(jnp.bfloat16)
        mixed = jnp.dot(weights, v_ref[0, :, lanes], preferred_element_type=jnp.float32)
        out_ref[:, 0, :, lanes] = mixed.astype(jnp.bfloat16).reshape(G, ROWS, HD)


def attend(picked, keys, values, lengths):
    slots, span, feats = keys.shape
    return pl.pallas_call(
        attend_kernel,
        out_shape=jax.ShapeDtypeStruct((G, slots, ROWS, feats), jnp.bfloat16),
        grid=(slots,),
        in_specs=[
            SMEM,
            pl.BlockSpec((G, G, 1, ROWS, feats // G), lambda s: (0, 0, s, 0, 0)),
            pl.BlockSpec((1, span, feats), lambda s: (s, 0, 0)),
            pl.BlockSpec((1, span, feats), lambda s: (s, 0, 0)),
        ],
        out_specs=pl.BlockSpec((G, 1, ROWS, feats), lambda s: (0, s, 0, 0)),
        compiler_params=PARAMS,
        cost_estimate=cost(4 * slots * STRETCH * span * feats, 4 * slots * span * feats),
        name="attend",
    )(lengths, picked, keys, values)


def project_kernel(a_ref, w_ref, out_ref):
    out_ref[0] = jnp.dot(a_ref[...], w_ref[...], preferred_element_type=jnp.float32).astype(
        jnp.bfloat16
    )


def project(rows, weight):
    m, k = rows.shape
    n = weight.shape[1]
    return pl.pallas_call(
        project_kernel,
        out_shape=jax.ShapeDtypeStruct((G, m, n // G), jnp.bfloat16),
        grid=(G,),
        in_specs=[
            pl.BlockSpec((m, k), lambda c: (0, 0)),
            pl.BlockSpec((k, n // G), lambda c: (0, c)),
        ],
        out_specs=pl.BlockSpec((1, m, n // G), lambda c: (c, 0, 0)),
        compiler_params=PARAMS,
        cost_estimate=cost(2 * m * n * k, 2 * (m * k + n * k + m * n)),
        name="project",
    )(rows, weight)


def sum_permute_kernel(order_ref, in_ref, out_ref):
    for place in range(out_ref.shape[0]):
        taken = order_ref[place]
        total = in_ref[0, taken].astype(jnp.float32)
        for part in range(1, in_ref.shape[0]):
            total = total + in_ref[part, taken].astype(jnp.float32)
        out_ref[place] = total.astype(out_ref.dtype)


def sum_permute(parts, order):
    return pl.pallas_call(
        sum_permute_kernel,
        out_shape=jax.ShapeDtypeStruct(parts.shape[1:], parts.dtype),
        in_specs=[SMEM, VMEM],
        out_specs=VMEM,
        compiler_params=PARAMS,
        cost_estimate=cost(parts.size, 3 * parts.size),
        name="sum_permute",
    )(order, parts)


def exchange(value, axes):
    return lax.all_to_all(value, axes, split_axis=0, concat_axis=0, tiled=True)


def local(queries, nb_keys, nb_values, nb_lengths, slot_stretch, out_weight, residual):
    per_dev = slot_stretch.shape[1]
    feats = queries.shape[2]
    part = feats // G
    sections = lax.axis_size("segment")
    count = per_dev * G * G
    back = [(i, (i - 1) % sections) for i in range(sections)]

    weight = lax.ppermute(out_weight[0], "segment", back)
    weight, first = lax.optimization_barrier((weight, queries[0]))
    weight = lax.all_gather(weight, "zh", axis=1, tiled=True)

    moved = lax.ppermute(first, "segment", back)
    pieces = moved.reshape(per_dev, G, ROWS, G, part).transpose(1, 3, 0, 2, 4)
    note = jnp.pad(slot_stretch.astype(jnp.bfloat16), ((0, 7), (0, part - per_dev)))
    pieces = jnp.concatenate(
        [
            pieces.reshape(G * G, per_dev * ROWS, part),
            jnp.broadcast_to(note[None], (G * G,) + note.shape),
        ],
        axis=1,
    )
    spread = exchange(pieces, SEQ)

    table = spread[:, per_dev * ROWS, :per_dev].astype(jnp.int32).reshape(count)
    ids = jnp.arange(count, dtype=jnp.int32)
    inverse = jnp.sum(jnp.where(table[None, :] == ids[:, None], ids[None, :], 0), axis=1)
    ordered = permute_blocks(spread, table, per_dev)
    picked = exchange(ordered.reshape(G * G, per_dev, ROWS, part), SEQ)

    answer = attend(
        picked.reshape(G, G, per_dev, ROWS, part), nb_keys[0], nb_values[0], nb_lengths[0]
    )
    banded = exchange(answer, "zh")
    everywhere = jnp.broadcast_to(banded[None], (G,) + banded.shape)
    gathered = exchange(everywhere, "x")

    partial = project(gathered.reshape(count * ROWS, feats), weight)
    partial = exchange(partial, "tp").reshape(G, count, ROWS, part)
    summed = sum_permute(partial, inverse)

    moves = []
    for s in range(sections):
        for x in range(G):
            for zh in range(G):
                for t in range(G):
                    source = ((s * G + x) * G + zh) * G + t
                    target = ((((s + 1) % sections) * G + t) * G + zh) * G + x
                    moves.append((source, target))
    turned = lax.ppermute(summed, ("segment", "x", "zh", "tp"), moves)
    owned = exchange(turned.reshape(G * G, per_dev, ROWS, part), SEQ)
    owned = owned.reshape(G, G, per_dev, ROWS, part).transpose(2, 1, 3, 0, 4)
    projected = owned.reshape(per_dev * STRETCH, feats).astype(jnp.float32)
    return (residual[0].astype(jnp.float32) + projected).astype(jnp.bfloat16)[None]


def solution(mesh):
    sections, _, tp = mesh.devices.shape
    inner = Mesh(mesh.devices.reshape(sections, G, G, tp), ("segment", "x", "zh", "tp"))
    in_specs = (
        P("segment", SEQ, "tp"),
        P("segment", SEQ, None, "tp"),
        P("segment", SEQ, None, "tp"),
        P("segment", SEQ, None),
        P("segment", SEQ),
        P("segment", "tp", SEQ),
        P("segment", SEQ, "tp"),
    )
    out_specs = P("segment", SEQ, "tp")
    return jax.shard_map(local, mesh=inner, in_specs=in_specs, out_specs=out_specs, check_vma=False)
```

```python
import functools
import math

import jax
import jax.numpy as jnp
from jax import lax
from jax.experimental import pallas as pl
from jax.experimental.pallas import tpu as pltpu
from jax.sharding import Mesh
from jax.sharding import PartitionSpec as P

HD = 128
STRETCH = 64
NR = 128
G = 4
ROWS = STRETCH // G
VMEM = pl.BlockSpec(memory_space=pltpu.VMEM)
SMEM = pl.BlockSpec(memory_space=pltpu.SMEM)
PARAMS = pltpu.CompilerParams(vmem_limit_bytes=40 * 1024 * 1024)
SEQ = ("x", "zh")
CHUNKS = 2


def cost(flops, moved, trans=0):
    return pl.CostEstimate(flops=flops, bytes_accessed=moved, transcendentals=trans)


def permute_kernel(per_dev, order_ref, in_ref, out_ref):
    for slot in range(out_ref.shape[0]):
        taken = order_ref[slot]
        start = pl.multiple_of(lax.rem(taken, per_dev) * ROWS, ROWS)
        out_ref[slot] = in_ref[lax.div(taken, per_dev), pl.ds(start, ROWS), :]


def permute_blocks(spread, order, per_dev):
    sources, _, part = spread.shape
    return pl.pallas_call(
        functools.partial(permute_kernel, per_dev),
        out_shape=jax.ShapeDtypeStruct((sources * per_dev, ROWS, part), spread.dtype),
        in_specs=[SMEM, VMEM],
        out_specs=VMEM,
        compiler_params=PARAMS,
        cost_estimate=cost(0, 4 * spread.size),
        name="permute_blocks",
    )(order, spread)


def attend_kernel(len_ref, q_ref, k_ref, v_ref, out_ref):
    slot = pl.program_id(0)
    span = k_ref.shape[1]
    heads = k_ref.shape[2] // HD
    groups = q_ref.shape[1]
    per_group = heads // groups
    position = lax.broadcasted_iota(jnp.int32, (1, span), 1)
    limit = jnp.where(position < NR, len_ref[slot, 0], len_ref[slot, 1] + NR)
    valid = position < limit
    lanes = [slice(head * HD, (head + 1) * HD) for head in range(heads)]
    scores = []
    for head in range(heads):
        part = slice((head % per_group) * HD, (head % per_group + 1) * HD)
        q = q_ref[:, head // per_group, 0, :, part].reshape(STRETCH, HD)
        scores.append(
            lax.dot_general(
                q,
                k_ref[0, :, lanes[head]],
                (((1,), (1,)), ((), ())),
                preferred_element_type=jnp.float32,
            )
        )
    weights = []
    for head in range(heads):
        masked = jnp.where(valid, scores[head] * (1.0 / math.sqrt(HD)), -1e30)
        expo = jnp.exp(masked - jnp.max(masked, axis=-1, keepdims=True))
        weights.append((expo / jnp.sum(expo, axis=-1, keepdims=True)).astype(jnp.bfloat16))
    for head in range(heads):
        mixed = jnp.dot(
            weights[head], v_ref[0, :, lanes[head]], preferred_element_type=jnp.float32
        )
        out_ref[:, 0, :, lanes[head]] = mixed.astype(jnp.bfloat16).reshape(G, ROWS, HD)


def attend(picked, keys, values, lengths, chunk, chunks):
    slots, span, feats = keys.shape
    wide = feats // chunks
    groups = G // chunks
    return pl.pallas_call(
        attend_kernel,
        out_shape=jax.ShapeDtypeStruct((G, slots, ROWS, wide), jnp.bfloat16),
        grid=(slots,),
        in_specs=[
            SMEM,
            pl.BlockSpec((G, groups, 1, ROWS, feats // G), lambda s: (0, chunk, s, 0, 0)),
            pl.BlockSpec((1, span, wide), lambda s: (s, 0, chunk)),
            pl.BlockSpec((1, span, wide), lambda s: (s, 0, chunk)),
        ],
        out_specs=pl.BlockSpec((G, 1, ROWS, wide), lambda s: (0, s, 0, 0)),
        compiler_params=PARAMS,
        cost_estimate=cost(4 * slots * STRETCH * span * wide, 4 * slots * span * wide),
        name="attend",
    )(lengths, picked, keys, values)


def project_kernel(chunks, order_ref, *refs):
    parts = len(refs[:-G - 1]) // chunks
    w_ref, outs = refs[-G - 1], refs[-G:]
    wide = refs[0].shape[1]
    for out, group in zip(outs, range(G)):
        taken = order_ref[group]
        start = 0
        for part in range(parts):
            rows = refs[part].shape[0]
            total = None
            for chunk in range(chunks):
                product = jnp.dot(
                    refs[chunk * parts + part][...],
                    w_ref[taken, chunk * wide : (chunk + 1) * wide, :],
                    preferred_element_type=jnp.float32,
                )
                total = product if total is None else total + product
            out[start : start + rows, :] = total.astype(jnp.bfloat16)
            start += rows


def project(parts, weight, order):
    chunks = len(parts)
    m = sum(p.shape[0] for p in parts[0])
    _, k, n = weight.shape
    flat = [p for chunk in parts for p in chunk]
    return pl.pallas_call(
        functools.partial(project_kernel, chunks),
        out_shape=[jax.ShapeDtypeStruct((m, n), jnp.bfloat16)] * G,
        in_specs=[SMEM] + [VMEM] * (len(flat) + 1),
        out_specs=[VMEM] * G,
        compiler_params=PARAMS,
        cost_estimate=cost(2 * m * n * k * G, 2 * (m * k + G * n * k + G * m * n)),
        name="project",
    )(order, *flat, weight)


def sum_permute_kernel(order_ref, *refs):
    out_ref = refs[-1]
    for place in range(out_ref.shape[0]):
        start = pl.multiple_of(order_ref[place] * ROWS, ROWS)
        total = None
        for ref in refs[:-1]:
            term = ref[pl.ds(start, ROWS), :].astype(jnp.float32)
            total = term if total is None else total + term
        out_ref[place] = total.astype(out_ref.dtype)


def sum_permute(parts, order):
    m, n = parts[0].shape
    return pl.pallas_call(
        sum_permute_kernel,
        out_shape=jax.ShapeDtypeStruct((m // ROWS, ROWS, n), parts[0].dtype),
        in_specs=[SMEM] + [VMEM] * len(parts),
        out_specs=VMEM,
        compiler_params=PARAMS,
        cost_estimate=cost(4 * m * n, 10 * m * n),
        name="sum_permute",
    )(order, *parts)


def exchange(value, axes):
    return lax.all_to_all(value, axes, split_axis=0, concat_axis=0, tiled=True)


def turn(value, axis, by):
    return lax.ppermute(value, axis, [(i, (i + by) % G) for i in range(G)])


def gather_ring(value):
    half = value.shape[0] // 2
    below = turn(value, "zh", 1)
    above = turn(value, "zh", -1)
    return [value, below, above, turn(below[:half], "zh", 1), turn(above[half:], "zh", -1)]


def local(queries, nb_keys, nb_values, nb_lengths, slot_stretch, out_weight, residual):
    per_dev = slot_stretch.shape[1]
    feats = queries.shape[2]
    part = feats // G
    sections = lax.axis_size("segment")
    count = per_dev * G * G
    back = [(i, (i - 1) % sections) for i in range(sections)]
    onward = [(i, (i + 1) % sections) for i in range(sections)]
    x, zh, t = lax.axis_index("x"), lax.axis_index("zh"), lax.axis_index("tp")

    moved = lax.ppermute(queries[0], "segment", back)
    pieces = moved.reshape(per_dev, G, ROWS, G, part).transpose(1, 3, 0, 2, 4)
    note = jnp.pad(slot_stretch.astype(jnp.bfloat16), ((0, 7), (0, part - per_dev)))
    pieces = jnp.concatenate(
        [
            pieces.reshape(G * G, per_dev * ROWS, part),
            jnp.broadcast_to(note[None], (G * G,) + note.shape),
        ],
        axis=1,
    )
    spread = exchange(pieces, SEQ)

    own = lax.ppermute(out_weight[0], "segment", back)
    weight = jnp.stack([own, turn(own, "x", -1), turn(own, "x", 2), turn(own, "x", 1)])

    table = spread[:, per_dev * ROWS, :per_dev].astype(jnp.int32).reshape(count)
    ids = jnp.arange(count, dtype=jnp.int32)
    holder, within = ids // per_dev, ids % per_dev
    apart = (holder % G - zh) % G
    rank = jnp.where(apart == 3, 1, jnp.where(apart == 1, 2, jnp.where(apart == 2, 3, 0)))
    place = (rank * G + holder // G) * per_dev + within
    places = jnp.sum(jnp.where(table[None, :] == ids[:, None], place[None, :], 0), axis=1)
    places = lax.ppermute(places, "segment", onward)

    ordered = permute_blocks(spread, table, per_dev)
    picked = exchange(ordered.reshape(G * G, per_dev, ROWS, part), SEQ)
    picked = picked.reshape(G, G, per_dev, ROWS, part)

    parts = []
    for chunk in range(CHUNKS):
        answer = attend(picked, nb_keys[0], nb_values[0], nb_lengths[0], chunk, CHUNKS)
        banded = exchange(answer, "x")
        parts.append(gather_ring(banded.reshape(-1, feats // CHUNKS)))

    order = (t + jnp.arange(G, dtype=jnp.int32) - x) % G
    partial = project(parts, weight, order)
    arrived = []
    for ahead, block in enumerate(partial):
        moves = []
        for s in range(sections):
            for i in range(G):
                moves.append((s * G + i, (s + 1) % sections * G + (i + ahead) % G))
        arrived.append(lax.ppermute(block, ("segment", "tp"), moves))
    summed = sum_permute(arrived, places)
    owned = exchange(summed.reshape(G * G, per_dev, ROWS, part), SEQ)
    owned = owned.reshape(G, G, per_dev, ROWS, part).transpose(2, 0, 3, 1, 4)
    projected = owned.reshape(per_dev * STRETCH, feats).astype(jnp.float32)
    return (residual[0].astype(jnp.float32) + projected).astype(jnp.bfloat16)[None]


def solution(mesh):
    sections, _, tp = mesh.devices.shape
    inner = Mesh(mesh.devices.reshape(sections, G, G, tp), ("segment", "x", "zh", "tp"))
    in_specs = (
        P("segment", SEQ, "tp"),
        P("segment", SEQ, None, "tp"),
        P("segment", SEQ, None, "tp"),
        P("segment", SEQ, None),
        P("segment", SEQ),
        P("segment", "tp", SEQ),
        P("segment", SEQ, "tp"),
    )
    out_specs = P("segment", SEQ, "tp")
    return jax.shard_map(local, mesh=inner, in_specs=in_specs, out_specs=out_specs, check_vma=False)
```

```python
import functools
import math

import jax
import jax.numpy as jnp
from jax import lax
from jax.experimental import pallas as pl
from jax.experimental.pallas import tpu as pltpu
from jax.sharding import Mesh
from jax.sharding import PartitionSpec as P

HD = 128
STRETCH = 64
NR = 128
G = 4
ROWS = STRETCH // G
VMEM = pl.BlockSpec(memory_space=pltpu.VMEM)
SMEM = pl.BlockSpec(memory_space=pltpu.SMEM)
PARAMS = pltpu.CompilerParams(vmem_limit_bytes=40 * 1024 * 1024)
SEQ = ("x", "zh")
CHUNKS = 1
AHEAD = (2, 3, 1, 0)


def cost(flops, moved, trans=0):
    return pl.CostEstimate(flops=flops, bytes_accessed=moved, transcendentals=trans)


def permute_kernel(per_dev, order_ref, in_ref, out_ref):
    for slot in range(out_ref.shape[0]):
        taken = order_ref[slot]
        start = pl.multiple_of(lax.rem(taken, per_dev) * ROWS, ROWS)
        out_ref[slot] = in_ref[lax.div(taken, per_dev), pl.ds(start, ROWS), :]


def permute_blocks(spread, order, per_dev):
    sources, _, part = spread.shape
    return pl.pallas_call(
        functools.partial(permute_kernel, per_dev),
        out_shape=jax.ShapeDtypeStruct((sources * per_dev, ROWS, part), spread.dtype),
        in_specs=[SMEM, VMEM],
        out_specs=VMEM,
        compiler_params=PARAMS,
        cost_estimate=cost(0, 4 * spread.size),
        name="permute_blocks",
    )(order, spread)


def attend_kernel(len_ref, q_ref, k_ref, v_ref, out_ref):
    slot = pl.program_id(0)
    span = k_ref.shape[1]
    heads = k_ref.shape[2] // HD
    groups = q_ref.shape[1]
    per_group = heads // groups
    position = lax.broadcasted_iota(jnp.int32, (1, span), 1)
    limit = jnp.where(position < NR, len_ref[slot, 0], len_ref[slot, 1] + NR)
    valid = position < limit
    lanes = [slice(head * HD, (head + 1) * HD) for head in range(heads)]
    scores = []
    for head in range(heads):
        part = slice((head % per_group) * HD, (head % per_group + 1) * HD)
        q = q_ref[:, head // per_group, 0, :, part].reshape(STRETCH, HD)
        scores.append(
            lax.dot_general(
                q,
                k_ref[0, :, lanes[head]],
                (((1,), (1,)), ((), ())),
                preferred_element_type=jnp.float32,
            )
        )
    weights = []
    for head in range(heads):
        masked = jnp.where(valid, scores[head] * (1.0 / math.sqrt(HD)), -1e30)
        expo = jnp.exp(masked - jnp.max(masked, axis=-1, keepdims=True))
        weights.append((expo / jnp.sum(expo, axis=-1, keepdims=True)).astype(jnp.bfloat16))
    for head in range(heads):
        mixed = jnp.dot(
            weights[head], v_ref[0, :, lanes[head]], preferred_element_type=jnp.float32
        )
        out_ref[:, 0, :, lanes[head]] = mixed.astype(jnp.bfloat16).reshape(G, ROWS, HD)


def attend(picked, keys, values, lengths, chunk, chunks):
    slots, span, feats = keys.shape
    wide = feats // chunks
    groups = G // chunks
    return pl.pallas_call(
        attend_kernel,
        out_shape=jax.ShapeDtypeStruct((G, slots, ROWS, wide), jnp.bfloat16),
        grid=(slots,),
        in_specs=[
            SMEM,
            pl.BlockSpec((G, groups, 1, ROWS, feats // G), lambda s: (0, chunk, s, 0, 0)),
            pl.BlockSpec((1, span, wide), lambda s: (s, 0, chunk)),
            pl.BlockSpec((1, span, wide), lambda s: (s, 0, chunk)),
        ],
        out_specs=pl.BlockSpec((G, 1, ROWS, wide), lambda s: (0, s, 0, 0)),
        compiler_params=PARAMS,
        cost_estimate=cost(4 * slots * STRETCH * span * wide, 4 * slots * span * wide),
        name="attend",
    )(lengths, picked, keys, values)


def project_kernel(chunks, order_ref, *refs):
    parts = len(refs[:-G - 1]) // chunks
    w_ref, outs = refs[-G - 1], refs[-G:]
    wide = refs[0].shape[1]
    for out, group in zip(outs, range(G)):
        taken = order_ref[group]
        start = 0
        for part in range(parts):
            rows = refs[part].shape[0]
            total = None
            for chunk in range(chunks):
                product = jnp.dot(
                    refs[chunk * parts + part][...],
                    w_ref[taken, chunk * wide : (chunk + 1) * wide, :],
                    preferred_element_type=jnp.float32,
                )
                total = product if total is None else total + product
            out[start : start + rows, :] = total.astype(jnp.bfloat16)
            start += rows


def project(parts, weight, order):
    chunks = len(parts)
    m = sum(p.shape[0] for p in parts[0])
    _, k, n = weight.shape
    flat = [p for chunk in parts for p in chunk]
    return pl.pallas_call(
        functools.partial(project_kernel, chunks),
        out_shape=[jax.ShapeDtypeStruct((m, n), jnp.bfloat16)] * G,
        in_specs=[SMEM] + [VMEM] * (len(flat) + 1),
        out_specs=[VMEM] * G,
        compiler_params=PARAMS,
        cost_estimate=cost(2 * m * n * k * G, 2 * (m * k + G * n * k + G * m * n)),
        name="project",
    )(order, *flat, weight)


def sum_permute_kernel(order_ref, *refs):
    out_ref = refs[-1]
    for place in range(out_ref.shape[0]):
        start = pl.multiple_of(order_ref[place] * ROWS, ROWS)
        total = None
        for ref in refs[:-1]:
            term = ref[pl.ds(start, ROWS), :].astype(jnp.float32)
            total = term if total is None else total + term
        out_ref[place] = total.astype(out_ref.dtype)


def sum_permute(parts, order):
    m, n = parts[0].shape
    return pl.pallas_call(
        sum_permute_kernel,
        out_shape=jax.ShapeDtypeStruct((m // ROWS, ROWS, n), parts[0].dtype),
        in_specs=[SMEM] + [VMEM] * len(parts),
        out_specs=VMEM,
        compiler_params=PARAMS,
        cost_estimate=cost(4 * m * n, 10 * m * n),
        name="sum_permute",
    )(order, *parts)


def exchange(value, axes):
    return lax.all_to_all(value, axes, split_axis=0, concat_axis=0, tiled=True)


def turn(value, axis, by):
    return lax.ppermute(value, axis, [(i, (i + by) % G) for i in range(G)])


def gather_ring(value):
    half = value.shape[0] // 2
    below = turn(value, "zh", 1)
    above = turn(value, "zh", -1)
    return [value, below, above, turn(below[:half], "zh", 1), turn(above[half:], "zh", -1)]


def local(queries, nb_keys, nb_values, nb_lengths, slot_stretch, out_weight, residual):
    per_dev = slot_stretch.shape[1]
    feats = queries.shape[2]
    part = feats // G
    sections = lax.axis_size("segment")
    count = per_dev * G * G
    back = [(i, (i - 1) % sections) for i in range(sections)]
    onward = [(i, (i + 1) % sections) for i in range(sections)]
    x, zh, t = lax.axis_index("x"), lax.axis_index("zh"), lax.axis_index("tp")

    moved = lax.ppermute(queries[0], "segment", back)
    pieces = moved.reshape(per_dev, G, ROWS, G, part).transpose(1, 3, 0, 2, 4)
    note = jnp.pad(slot_stretch.astype(jnp.bfloat16), ((0, 7), (0, part - per_dev)))
    pieces = jnp.concatenate(
        [
            pieces.reshape(G * G, per_dev * ROWS, part),
            jnp.broadcast_to(note[None], (G * G,) + note.shape),
        ],
        axis=1,
    )
    spread = exchange(pieces, SEQ)

    own = lax.ppermute(out_weight[0], "segment", back)

    table = spread[:, per_dev * ROWS, :per_dev].astype(jnp.int32).reshape(count)
    ids = jnp.arange(count, dtype=jnp.int32)
    holder, within = ids // per_dev, ids % per_dev
    apart = (holder % G - zh) % G
    rank = jnp.where(apart == 3, 1, jnp.where(apart == 1, 2, jnp.where(apart == 2, 3, 0)))
    place = (rank * G + holder // G) * per_dev + within
    places = jnp.sum(jnp.where(table[None, :] == ids[:, None], place[None, :], 0), axis=1)
    places = lax.ppermute(places, "segment", onward)

    ordered = permute_blocks(spread, table, per_dev)
    picked = exchange(ordered.reshape(G * G, per_dev, ROWS, part), SEQ)
    picked, places, own = lax.optimization_barrier((picked, places, own))
    picked = picked.reshape(G, G, per_dev, ROWS, part)

    parts = []
    for chunk in range(CHUNKS):
        answer = attend(picked, nb_keys[0], nb_values[0], nb_lengths[0], chunk, CHUNKS)
        banded = exchange(answer, "x")
        banded, own = lax.optimization_barrier((banded, own))
        weight = jnp.stack([own, turn(own, "x", -1), turn(own, "x", 2), turn(own, "x", 1)])
        parts.append(gather_ring(banded.reshape(-1, feats // CHUNKS)))

    order = (t + jnp.array(AHEAD, dtype=jnp.int32) - x) % G
    partial = project(parts, weight, order)
    arrived = []
    for ahead, block in zip(AHEAD, partial):
        moves = []
        for s in range(sections):
            for i in range(G):
                moves.append((s * G + i, (s + 1) % sections * G + (i + ahead) % G))
        arrived.append(lax.ppermute(block, ("segment", "tp"), moves))
    summed = sum_permute(arrived, places)
    owned = exchange(summed.reshape(G * G, per_dev, ROWS, part), SEQ)
    owned = owned.reshape(G, G, per_dev, ROWS, part).transpose(2, 0, 3, 1, 4)
    projected = owned.reshape(per_dev * STRETCH, feats).astype(jnp.float32)
    return (residual[0].astype(jnp.float32) + projected).astype(jnp.bfloat16)[None]


def solution(mesh):
    sections, _, tp = mesh.devices.shape
    inner = Mesh(mesh.devices.reshape(sections, G, G, tp), ("segment", "x", "zh", "tp"))
    in_specs = (
        P("segment", SEQ, "tp"),
        P("segment", SEQ, None, "tp"),
        P("segment", SEQ, None, "tp"),
        P("segment", SEQ, None),
        P("segment", SEQ),
        P("segment", "tp", SEQ),
        P("segment", SEQ, "tp"),
    )
    out_specs = P("segment", SEQ, "tp")
    return jax.shard_map(local, mesh=inner, in_specs=in_specs, out_specs=out_specs, check_vma=False)
```

```python
import functools
import math

import jax
import jax.numpy as jnp
from jax import lax
from jax.experimental import pallas as pl
from jax.experimental.pallas import tpu as pltpu
from jax.sharding import Mesh
from jax.sharding import PartitionSpec as P

HD = 128
STRETCH = 64
NR = 128
G = 4
ROWS = STRETCH // G
VMEM = pl.BlockSpec(memory_space=pltpu.VMEM)
SMEM = pl.BlockSpec(memory_space=pltpu.SMEM)
PARAMS = pltpu.CompilerParams(vmem_limit_bytes=40 * 1024 * 1024)
SEQ = ("x", "zh")
NOTE = 8
CHUNKS = 1
AHEAD = (2, 1, 3, 0)


def cost(flops, moved, trans=0):
    return pl.CostEstimate(flops=flops, bytes_accessed=moved, transcendentals=trans)


def permute_kernel(per_dev, order_ref, in_ref, out_ref):
    for slot in range(out_ref.shape[0]):
        taken = order_ref[slot]
        rows = out_ref.shape[1]
        start = pl.multiple_of(lax.rem(taken, per_dev) * rows, rows)
        out_ref[slot] = in_ref[lax.div(taken, per_dev), pl.ds(start, rows), :]


def permute_blocks(spread, order, per_dev):
    sources, _, lanes = spread.shape
    rows = (spread.shape[1] - NOTE) // per_dev
    return pl.pallas_call(
        functools.partial(permute_kernel, per_dev),
        out_shape=jax.ShapeDtypeStruct((sources * per_dev, rows, lanes), spread.dtype),
        in_specs=[SMEM, VMEM],
        out_specs=VMEM,
        compiler_params=PARAMS,
        cost_estimate=cost(0, 4 * spread.size),
        name="permute_blocks",
    )(order, spread)


def attend_kernel(len_ref, q_ref, k_ref, v_ref, out_ref):
    slot = pl.program_id(0)
    span = k_ref.shape[1]
    heads = k_ref.shape[2] // HD
    groups = q_ref.shape[1]
    per_group = heads // groups
    position = lax.broadcasted_iota(jnp.int32, (1, span), 1)
    limit = jnp.where(position < NR, len_ref[slot, 0], len_ref[slot, 1] + NR)
    valid = position < limit
    lanes = [slice(head * HD, (head + 1) * HD) for head in range(heads)]
    scores = []
    for head in range(heads):
        q = q_ref[:, head // per_group, 0, head % per_group].reshape(STRETCH, HD)
        scores.append(
            lax.dot_general(
                q,
                k_ref[0, :, lanes[head]],
                (((1,), (1,)), ((), ())),
                preferred_element_type=jnp.float32,
            )
        )
    weights = []
    for head in range(heads):
        masked = jnp.where(valid, scores[head] * (1.0 / math.sqrt(HD)), -1e30)
        expo = jnp.exp(masked - jnp.max(masked, axis=-1, keepdims=True))
        weights.append((expo / jnp.sum(expo, axis=-1, keepdims=True)).astype(jnp.bfloat16))
    for head in range(heads):
        mixed = jnp.dot(
            weights[head], v_ref[0, :, lanes[head]], preferred_element_type=jnp.float32
        )
        out_ref[:, 0, :, lanes[head]] = mixed.astype(jnp.bfloat16).reshape(G, ROWS, HD)


def attend(picked, keys, values, lengths, chunk, chunks):
    slots, span, feats = keys.shape
    wide = feats // chunks
    groups = G // chunks
    return pl.pallas_call(
        attend_kernel,
        out_shape=jax.ShapeDtypeStruct((G, slots, ROWS, wide), jnp.bfloat16),
        grid=(slots,),
        in_specs=[
            SMEM,
            pl.BlockSpec((G, groups, 1, feats // G // HD, ROWS, HD), lambda s: (0, chunk, s, 0, 0, 0)),
            pl.BlockSpec((1, span, wide), lambda s: (s, 0, chunk)),
            pl.BlockSpec((1, span, wide), lambda s: (s, 0, chunk)),
        ],
        out_specs=pl.BlockSpec((G, 1, ROWS, wide), lambda s: (0, s, 0, 0)),
        compiler_params=PARAMS,
        cost_estimate=cost(4 * slots * STRETCH * span * wide, 4 * slots * span * wide),
        name="attend",
    )(lengths, picked, keys, values)


def project_kernel(chunks, order_ref, *refs):
    parts = len(refs[:-G - 1]) // chunks
    w_ref, outs = refs[-G - 1], refs[-G:]
    wide = refs[0].shape[1]
    for out, group in zip(outs, range(G)):
        taken = order_ref[group]
        start = 0
        for part in range(parts):
            rows = refs[part].shape[0]
            total = None
            for chunk in range(chunks):
                product = jnp.dot(
                    refs[chunk * parts + part][...],
                    w_ref[taken, chunk * wide : (chunk + 1) * wide, :],
                    preferred_element_type=jnp.float32,
                )
                total = product if total is None else total + product
            out[start : start + rows, :] = total.astype(jnp.bfloat16)
            start += rows


def project(parts, weight, order):
    chunks = len(parts)
    m = sum(p.shape[0] for p in parts[0])
    _, k, n = weight.shape
    flat = [p for chunk in parts for p in chunk]
    return pl.pallas_call(
        functools.partial(project_kernel, chunks),
        out_shape=[jax.ShapeDtypeStruct((m, n), jnp.bfloat16)] * G,
        in_specs=[SMEM] + [VMEM] * (len(flat) + 1),
        out_specs=[VMEM] * G,
        compiler_params=PARAMS,
        cost_estimate=cost(2 * m * n * k * G, 2 * (m * k + G * n * k + G * m * n)),
        name="project",
    )(order, *flat, weight)


def sum_permute_kernel(order_ref, *refs):
    out_ref = refs[-1]
    for place in range(out_ref.shape[0]):
        start = pl.multiple_of(order_ref[place] * ROWS, ROWS)
        total = None
        for ref in refs[:-1]:
            term = ref[pl.ds(start, ROWS), :].astype(jnp.float32)
            total = term if total is None else total + term
        out_ref[place] = total.astype(out_ref.dtype)


def sum_permute(parts, order):
    m, n = parts[0].shape
    return pl.pallas_call(
        sum_permute_kernel,
        out_shape=jax.ShapeDtypeStruct((m // ROWS, ROWS, n), parts[0].dtype),
        in_specs=[SMEM] + [VMEM] * len(parts),
        out_specs=VMEM,
        compiler_params=PARAMS,
        cost_estimate=cost(4 * m * n, 10 * m * n),
        name="sum_permute",
    )(order, *parts)


def finish_kernel(in_ref, residual_ref, out_ref):
    _, per_dev, rows, part = in_ref.shape
    for x in range(G):
        for zh in range(G):
            for within in range(per_dev):
                start = (within * G + x) * rows
                here = (slice(start, start + rows), slice(zh * part, (zh + 1) * part))
                total = residual_ref[here].astype(jnp.float32)
                total = total + in_ref[x * G + zh, within].astype(jnp.float32)
                out_ref[here] = total.astype(out_ref.dtype)


def finish(owned, residual):
    return pl.pallas_call(
        finish_kernel,
        out_shape=jax.ShapeDtypeStruct(residual.shape, residual.dtype),
        in_specs=[VMEM, VMEM],
        out_specs=VMEM,
        compiler_params=PARAMS,
        cost_estimate=cost(residual.size, 6 * residual.size),
        name="finish",
    )(owned, residual)


def exchange(value, axes):
    return lax.all_to_all(value, axes, split_axis=0, concat_axis=0, tiled=True)


def turn(value, axis, by):
    return lax.ppermute(value, axis, [(i, (i + by) % G) for i in range(G)])


def gather_ring(value):
    half = value.shape[0] // 2
    below = turn(value, "zh", 1)
    above = turn(value, "zh", -1)
    return [value, below, above, turn(below[:half], "zh", 1), turn(above[half:], "zh", -1)]


def local(queries, nb_keys, nb_values, nb_lengths, slot_stretch, out_weight, residual):
    per_dev = slot_stretch.shape[1]
    feats = queries.shape[2]
    part = feats // G
    sections = lax.axis_size("segment")
    count = per_dev * G * G
    back = [(i, (i - 1) % sections) for i in range(sections)]
    onward = [(i, (i + 1) % sections) for i in range(sections)]
    x, zh, t = lax.axis_index("x"), lax.axis_index("zh"), lax.axis_index("tp")

    moved = lax.ppermute(queries[0], "segment", back)
    pair = part // HD
    pieces = moved.reshape(per_dev, G, ROWS, G, pair, HD).transpose(1, 3, 0, 4, 2, 5)
    note = jnp.pad(slot_stretch.astype(jnp.bfloat16), ((0, NOTE - 1), (0, HD - per_dev)))
    pieces = jnp.concatenate(
        [
            pieces.reshape(G * G, per_dev * pair * ROWS, HD),
            jnp.broadcast_to(note[None], (G * G,) + note.shape),
        ],
        axis=1,
    )
    spread = exchange(pieces, SEQ)

    own = lax.ppermute(out_weight[0], "segment", back)

    table = spread[:, per_dev * pair * ROWS, :per_dev].astype(jnp.int32).reshape(count)
    ids = jnp.arange(count, dtype=jnp.int32)
    holder, within = ids // per_dev, ids % per_dev
    apart = (holder % G - zh) % G
    rank = jnp.where(apart == 3, 1, jnp.where(apart == 1, 2, jnp.where(apart == 2, 3, 0)))
    place = (rank * G + holder // G) * per_dev + within
    places = jnp.sum(jnp.where(table[None, :] == ids[:, None], place[None, :], 0), axis=1)
    places = lax.ppermute(places, "segment", onward)

    ordered = permute_blocks(spread, table, per_dev)
    picked = exchange(ordered.reshape(G * G, per_dev, pair * ROWS, HD), SEQ)
    picked, places, own = lax.optimization_barrier((picked, places, own))
    picked = picked.reshape(G, G, per_dev, pair, ROWS, HD)

    parts = []
    for chunk in range(CHUNKS):
        answer = attend(picked, nb_keys[0], nb_values[0], nb_lengths[0], chunk, CHUNKS)
        banded = exchange(answer, "x")
        banded, own = lax.optimization_barrier((banded, own))
        weight = jnp.stack([own, turn(own, "x", -1), turn(own, "x", 2), turn(own, "x", 1)])
        parts.append(gather_ring(banded.reshape(-1, feats // CHUNKS)))

    order = (t + jnp.array(AHEAD, dtype=jnp.int32) - x) % G
    partial = project(parts, weight, order)
    arrived = []
    for ahead, block in zip(AHEAD, partial):
        moves = []
        for s in range(sections):
            for i in range(G):
                moves.append((s * G + i, (s + 1) % sections * G + (i + ahead) % G))
        arrived.append(lax.ppermute(block, ("segment", "tp"), moves))
    summed = sum_permute(arrived, places)
    owned = exchange(summed.reshape(G * G, per_dev, ROWS, part), SEQ)
    return finish(owned, residual[0])[None]


def solution(mesh):
    sections, _, tp = mesh.devices.shape
    inner = Mesh(mesh.devices.reshape(sections, G, G, tp), ("segment", "x", "zh", "tp"))
    in_specs = (
        P("segment", SEQ, "tp"),
        P("segment", SEQ, None, "tp"),
        P("segment", SEQ, None, "tp"),
        P("segment", SEQ, None),
        P("segment", SEQ),
        P("segment", "tp", SEQ),
        P("segment", SEQ, "tp"),
    )
    out_specs = P("segment", SEQ, "tp")
    return jax.shard_map(local, mesh=inner, in_specs=in_specs, out_specs=out_specs, check_vma=False)
```

```python
import functools
import math

import jax
import jax.numpy as jnp
from jax import lax
from jax.experimental import pallas as pl
from jax.experimental.pallas import tpu as pltpu
from jax.sharding import Mesh
from jax.sharding import PartitionSpec as P

HD = 128
STRETCH = 64
NR = 128
G = 4
ROWS = STRETCH // G
VMEM = pl.BlockSpec(memory_space=pltpu.VMEM)
SMEM = pl.BlockSpec(memory_space=pltpu.SMEM)
PARAMS = pltpu.CompilerParams(vmem_limit_bytes=40 * 1024 * 1024)
SEQ = ("x", "zh")
NOTE = 8
CHUNKS = 1
AHEAD = (2, 1, 3, 0)
FORWARD = 16


def cost(flops, moved, trans=0):
    return pl.CostEstimate(flops=flops, bytes_accessed=moved, transcendentals=trans)


def permute_kernel(per_dev, order_ref, in_ref, out_ref):
    for slot in range(out_ref.shape[0]):
        taken = order_ref[slot]
        rows = out_ref.shape[1]
        start = pl.multiple_of(lax.rem(taken, per_dev) * rows, rows)
        out_ref[slot] = in_ref[lax.div(taken, per_dev), pl.ds(start, rows), :]


def permute_blocks(spread, order, per_dev):
    sources, _, lanes = spread.shape
    rows = (spread.shape[1] - NOTE) // per_dev
    return pl.pallas_call(
        functools.partial(permute_kernel, per_dev),
        out_shape=jax.ShapeDtypeStruct((sources * per_dev, rows, lanes), spread.dtype),
        in_specs=[SMEM, VMEM],
        out_specs=VMEM,
        compiler_params=PARAMS,
        cost_estimate=cost(0, 4 * spread.size),
        name="permute_blocks",
    )(order, spread)


def attend_kernel(len_ref, q_ref, k_ref, v_ref, out_ref):
    slot = pl.program_id(0)
    span = k_ref.shape[1]
    heads = k_ref.shape[2] // HD
    groups = q_ref.shape[1]
    per_group = heads // groups
    position = lax.broadcasted_iota(jnp.int32, (1, span), 1)
    limit = jnp.where(position < NR, len_ref[slot, 0], len_ref[slot, 1] + NR)
    valid = position < limit
    lanes = [slice(head * HD, (head + 1) * HD) for head in range(heads)]
    scores = []
    for head in range(heads):
        q = q_ref[:, head // per_group, 0, head % per_group].reshape(STRETCH, HD)
        scores.append(
            lax.dot_general(
                q,
                k_ref[0, :, lanes[head]],
                (((1,), (1,)), ((), ())),
                preferred_element_type=jnp.float32,
            )
        )
    weights = []
    for head in range(heads):
        masked = jnp.where(valid, scores[head] * (1.0 / math.sqrt(HD)), -1e30)
        expo = jnp.exp(masked - jnp.max(masked, axis=-1, keepdims=True))
        weights.append((expo / jnp.sum(expo, axis=-1, keepdims=True)).astype(jnp.bfloat16))
    for head in range(heads):
        mixed = jnp.dot(
            weights[head], v_ref[0, :, lanes[head]], preferred_element_type=jnp.float32
        )
        out_ref[:, 0, :, lanes[head]] = mixed.astype(jnp.bfloat16).reshape(G, ROWS, HD)


def attend(picked, keys, values, lengths, chunk, chunks):
    slots, span, feats = keys.shape
    wide = feats // chunks
    groups = G // chunks
    return pl.pallas_call(
        attend_kernel,
        out_shape=jax.ShapeDtypeStruct((G, slots, ROWS, wide), jnp.bfloat16),
        grid=(slots,),
        in_specs=[
            SMEM,
            pl.BlockSpec((G, groups, 1, feats // G // HD, ROWS, HD), lambda s: (0, chunk, s, 0, 0, 0)),
            pl.BlockSpec((1, span, wide), lambda s: (s, 0, chunk)),
            pl.BlockSpec((1, span, wide), lambda s: (s, 0, chunk)),
        ],
        out_specs=pl.BlockSpec((G, 1, ROWS, wide), lambda s: (0, s, 0, 0)),
        compiler_params=PARAMS,
        cost_estimate=cost(4 * slots * STRETCH * span * wide, 4 * slots * span * wide),
        name="attend",
    )(lengths, picked, keys, values)


def project_kernel(order_ref, *refs):
    blocks, weights, outs = refs[: -2 * G], refs[-2 * G : -G], refs[-G:]

    def fill(out, w_ref):
        start = 0
        for ref in blocks:
            product = jnp.dot(ref[...], w_ref[...], preferred_element_type=jnp.float32)
            out[start : start + ref.shape[0], :] = product.astype(jnp.bfloat16)
            start += ref.shape[0]

    for group, out in enumerate(outs):
        for distance, w_ref in enumerate(weights):
            pl.when(order_ref[group] == distance)(functools.partial(fill, out, w_ref))


def project(blocks, weights, order):
    m = sum(block.shape[0] for block in blocks)
    k, n = weights[0].shape
    return pl.pallas_call(
        project_kernel,
        out_shape=[jax.ShapeDtypeStruct((m, n), jnp.bfloat16)] * G,
        in_specs=[SMEM] + [VMEM] * (len(blocks) + G),
        out_specs=[VMEM] * G,
        compiler_params=PARAMS,
        cost_estimate=cost(2 * m * n * k * G, 2 * (m * k + G * n * k + G * m * n)),
        name="project",
    )(order, *blocks, *weights)


def sum_permute_kernel(order_ref, *refs):
    out_ref = refs[-1]
    for place in range(out_ref.shape[0]):
        start = pl.multiple_of(order_ref[place] * ROWS, ROWS)
        total = None
        for ref in refs[:-1]:
            term = ref[pl.ds(start, ROWS), :].astype(jnp.float32)
            total = term if total is None else total + term
        out_ref[place] = total.astype(out_ref.dtype)


def sum_permute(parts, order):
    m, n = parts[0].shape
    return pl.pallas_call(
        sum_permute_kernel,
        out_shape=jax.ShapeDtypeStruct((m // ROWS, ROWS, n), parts[0].dtype),
        in_specs=[SMEM] + [VMEM] * len(parts),
        out_specs=VMEM,
        compiler_params=PARAMS,
        cost_estimate=cost(4 * m * n, 10 * m * n),
        name="sum_permute",
    )(order, *parts)


def finish_kernel(in_ref, residual_ref, out_ref):
    _, per_dev, rows, part = in_ref.shape
    for x in range(G):
        for zh in range(G):
            for within in range(per_dev):
                start = (within * G + x) * rows
                here = (slice(start, start + rows), slice(zh * part, (zh + 1) * part))
                total = residual_ref[here].astype(jnp.float32)
                total = total + in_ref[x * G + zh, within].astype(jnp.float32)
                out_ref[here] = total.astype(out_ref.dtype)


def finish(owned, residual):
    return pl.pallas_call(
        finish_kernel,
        out_shape=jax.ShapeDtypeStruct(residual.shape, residual.dtype),
        in_specs=[VMEM, VMEM],
        out_specs=VMEM,
        compiler_params=PARAMS,
        cost_estimate=cost(residual.size, 6 * residual.size),
        name="finish",
    )(owned, residual)


def exchange(value, axes):
    return lax.all_to_all(value, axes, split_axis=0, concat_axis=0, tiled=True)


def turn(value, axis, by):
    return lax.ppermute(value, axis, [(i, (i + by) % G) for i in range(G)])


def gather_ring(value):
    half = value.shape[0] // 2 + FORWARD
    below = turn(value, "zh", 1)
    above = turn(value, "zh", -1)
    return [value, below, above, turn(below[:half], "zh", 1), turn(above[half:], "zh", -1)]


def local(queries, nb_keys, nb_values, nb_lengths, slot_stretch, out_weight, residual):
    per_dev = slot_stretch.shape[1]
    feats = queries.shape[2]
    part = feats // G
    sections = lax.axis_size("segment")
    count = per_dev * G * G
    back = [(i, (i - 1) % sections) for i in range(sections)]
    onward = [(i, (i + 1) % sections) for i in range(sections)]
    x, zh, t = lax.axis_index("x"), lax.axis_index("zh"), lax.axis_index("tp")

    moved = lax.ppermute(queries[0], "segment", back)
    pair = part // HD
    pieces = moved.reshape(per_dev, G, ROWS, G, pair, HD).transpose(1, 3, 0, 4, 2, 5)
    note = jnp.pad(slot_stretch.astype(jnp.bfloat16), ((0, NOTE - 1), (0, HD - per_dev)))
    pieces = jnp.concatenate(
        [
            pieces.reshape(G * G, per_dev * pair * ROWS, HD),
            jnp.broadcast_to(note[None], (G * G,) + note.shape),
        ],
        axis=1,
    )
    spread = exchange(pieces, SEQ)

    own = lax.ppermute(out_weight[0], "segment", back)

    table = spread[:, per_dev * pair * ROWS, :per_dev].astype(jnp.int32).reshape(count)
    ids = jnp.arange(count, dtype=jnp.int32)
    holder, within = ids // per_dev, ids % per_dev
    apart = (holder % G - zh) % G
    rank = jnp.where(apart == 3, 1, jnp.where(apart == 1, 2, jnp.where(apart == 2, 3, 0)))
    place = (rank * G + holder // G) * per_dev + within
    places = jnp.sum(jnp.where(table[None, :] == ids[:, None], place[None, :], 0), axis=1)
    places = lax.ppermute(places, "segment", onward)

    ordered = permute_blocks(spread, table, per_dev)
    picked = exchange(ordered.reshape(G * G, per_dev, pair * ROWS, HD), SEQ)
    picked, places, own = lax.optimization_barrier((picked, places, own))
    picked = picked.reshape(G, G, per_dev, pair, ROWS, HD)

    parts = []
    for chunk in range(CHUNKS):
        answer = attend(picked, nb_keys[0], nb_values[0], nb_lengths[0], chunk, CHUNKS)
        banded = exchange(answer, "x")
        banded, own = lax.optimization_barrier((banded, own))
        weight = [own, turn(own, "x", -1), turn(own, "x", 2), turn(own, "x", 1)]
        parts.append(gather_ring(banded.reshape(-1, feats // CHUNKS)))

    order = (t + jnp.array(AHEAD, dtype=jnp.int32) - x) % G
    partial = project(parts[0], weight, order)
    arrived = []
    for ahead, block in zip(AHEAD, partial):
        moves = []
        for s in range(sections):
            for i in range(G):
                moves.append((s * G + i, (s + 1) % sections * G + (i + ahead) % G))
        arrived.append(lax.ppermute(block, ("segment", "tp"), moves))
    summed = sum_permute(arrived, places)
    owned = exchange(summed.reshape(G * G, per_dev, ROWS, part), SEQ)
    return finish(owned, residual[0])[None]


def solution(mesh):
    sections, _, tp = mesh.devices.shape
    inner = Mesh(mesh.devices.reshape(sections, G, G, tp), ("segment", "x", "zh", "tp"))
    in_specs = (
        P("segment", SEQ, "tp"),
        P("segment", SEQ, None, "tp"),
        P("segment", SEQ, None, "tp"),
        P("segment", SEQ, None),
        P("segment", SEQ),
        P("segment", "tp", SEQ),
        P("segment", SEQ, "tp"),
    )
    out_specs = P("segment", SEQ, "tp")
    return jax.shard_map(local, mesh=inner, in_specs=in_specs, out_specs=out_specs, check_vma=False)
```

```python
import functools
import math

import jax
import jax.numpy as jnp
from jax import lax
from jax.experimental import pallas as pl
from jax.experimental.pallas import tpu as pltpu
from jax.sharding import Mesh
from jax.sharding import PartitionSpec as P

HD = 128
STRETCH = 64
NR = 128
G = 4
ROWS = STRETCH // G
VMEM = pl.BlockSpec(memory_space=pltpu.VMEM)
SMEM = pl.BlockSpec(memory_space=pltpu.SMEM)
PARAMS = pltpu.CompilerParams(vmem_limit_bytes=40 * 1024 * 1024)
SEQ = ("x", "zh")
NOTE = 8
CHUNKS = 1
AHEAD = (2, 1, 3, 0)
FORWARD = 16


def cost(flops, moved, trans=0):
    return pl.CostEstimate(flops=flops, bytes_accessed=moved, transcendentals=trans)


def permute_kernel(per_dev, order_ref, in_ref, out_ref):
    for slot in range(out_ref.shape[0]):
        taken = order_ref[slot]
        rows = out_ref.shape[1]
        start = pl.multiple_of(lax.rem(taken, per_dev) * rows, rows)
        out_ref[slot] = in_ref[lax.div(taken, per_dev), pl.ds(start, rows), :]


def permute_blocks(spread, order, per_dev):
    sources, _, lanes = spread.shape
    rows = (spread.shape[1] - NOTE) // per_dev
    return pl.pallas_call(
        functools.partial(permute_kernel, per_dev),
        out_shape=jax.ShapeDtypeStruct((sources * per_dev, rows, lanes), spread.dtype),
        in_specs=[SMEM, VMEM],
        out_specs=VMEM,
        compiler_params=PARAMS,
        cost_estimate=cost(0, 4 * spread.size),
        name="permute_blocks",
    )(order, spread)


def attend_kernel(len_ref, q_ref, k_ref, values_ref, out_ref, held_ref, sem):
    slot = pl.program_id(0)
    slots = held_ref.shape[0]

    @pl.when(slot == 0)
    def _():
        for each in range(slots):
            pltpu.make_async_copy(values_ref.at[each], held_ref.at[each], sem.at[each]).start()

    span = k_ref.shape[1]
    heads = k_ref.shape[2] // HD
    groups = q_ref.shape[1]
    per_group = heads // groups
    position = lax.broadcasted_iota(jnp.int32, (1, span), 1)
    limit = jnp.where(position < NR, len_ref[slot, 0], len_ref[slot, 1] + NR)
    valid = position < limit
    lanes = [slice(head * HD, (head + 1) * HD) for head in range(heads)]
    scores = []
    for head in range(heads):
        q = q_ref[:, head // per_group, 0, head % per_group].reshape(STRETCH, HD)
        scores.append(
            lax.dot_general(
                q,
                k_ref[0, :, lanes[head]],
                (((1,), (1,)), ((), ())),
                preferred_element_type=jnp.float32,
            )
        )
    weights = []
    for head in range(heads):
        masked = jnp.where(valid, scores[head] * (1.0 / math.sqrt(HD)), -1e30)
        expo = jnp.exp(masked - jnp.max(masked, axis=-1, keepdims=True))
        weights.append((expo / jnp.sum(expo, axis=-1, keepdims=True)).astype(jnp.bfloat16))
    pltpu.make_async_copy(values_ref.at[slot], held_ref.at[slot], sem.at[slot]).wait()
    for head in range(heads):
        mixed = jnp.dot(
            weights[head], held_ref[slot, :, lanes[head]], preferred_element_type=jnp.float32
        )
        out_ref[:, 0, :, lanes[head]] = mixed.astype(jnp.bfloat16).reshape(G, ROWS, HD)


def attend(picked, keys, values, lengths, chunk, chunks):
    slots, span, feats = keys.shape
    wide = feats // chunks
    groups = G // chunks
    return pl.pallas_call(
        attend_kernel,
        out_shape=jax.ShapeDtypeStruct((G, slots, ROWS, wide), jnp.bfloat16),
        grid=(slots,),
        in_specs=[
            SMEM,
            pl.BlockSpec((G, groups, 1, feats // G // HD, ROWS, HD), lambda s: (0, chunk, s, 0, 0, 0)),
            pl.BlockSpec((1, span, wide), lambda s: (s, 0, chunk)),
            pl.BlockSpec(memory_space=pltpu.HBM),
        ],
        out_specs=pl.BlockSpec((G, 1, ROWS, wide), lambda s: (0, s, 0, 0)),
        scratch_shapes=[
            pltpu.VMEM((slots, span, wide), values.dtype),
            pltpu.SemaphoreType.DMA((slots,)),
        ],
        compiler_params=PARAMS,
        cost_estimate=cost(4 * slots * STRETCH * span * wide, 4 * slots * span * wide),
        name="attend",
    )(lengths, picked, keys, values)


def project_kernel(order_ref, *refs):
    blocks, weights, outs = refs[: -2 * G], refs[-2 * G : -G], refs[-G:]

    def fill(out, w_ref):
        start = 0
        for ref in blocks:
            product = jnp.dot(ref[...], w_ref[...], preferred_element_type=jnp.float32)
            out[start : start + ref.shape[0], :] = product.astype(jnp.bfloat16)
            start += ref.shape[0]

    for group, out in enumerate(outs):
        for distance, w_ref in enumerate(weights):
            pl.when(order_ref[group] == distance)(functools.partial(fill, out, w_ref))


def project(blocks, weights, order):
    m = sum(block.shape[0] for block in blocks)
    k, n = weights[0].shape
    return pl.pallas_call(
        project_kernel,
        out_shape=[jax.ShapeDtypeStruct((m, n), jnp.bfloat16)] * G,
        in_specs=[SMEM] + [VMEM] * (len(blocks) + G),
        out_specs=[VMEM] * G,
        compiler_params=PARAMS,
        cost_estimate=cost(2 * m * n * k * G, 2 * (m * k + G * n * k + G * m * n)),
        name="project",
    )(order, *blocks, *weights)


def sum_permute_kernel(order_ref, *refs):
    out_ref = refs[-1]
    for place in range(out_ref.shape[0]):
        start = pl.multiple_of(order_ref[place] * ROWS, ROWS)
        total = None
        for ref in refs[:-1]:
            term = ref[pl.ds(start, ROWS), :].astype(jnp.float32)
            total = term if total is None else total + term
        out_ref[place] = total.astype(out_ref.dtype)


def sum_permute(parts, order):
    m, n = parts[0].shape
    return pl.pallas_call(
        sum_permute_kernel,
        out_shape=jax.ShapeDtypeStruct((m // ROWS, ROWS, n), parts[0].dtype),
        in_specs=[SMEM] + [VMEM] * len(parts),
        out_specs=VMEM,
        compiler_params=PARAMS,
        cost_estimate=cost(4 * m * n, 10 * m * n),
        name="sum_permute",
    )(order, *parts)


def finish_kernel(in_ref, residual_ref, out_ref):
    _, per_dev, rows, part = in_ref.shape
    for x in range(G):
        for zh in range(G):
            for within in range(per_dev):
                start = (within * G + x) * rows
                here = (slice(start, start + rows), slice(zh * part, (zh + 1) * part))
                total = residual_ref[here].astype(jnp.float32)
                total = total + in_ref[x * G + zh, within].astype(jnp.float32)
                out_ref[here] = total.astype(out_ref.dtype)


def finish(owned, residual):
    return pl.pallas_call(
        finish_kernel,
        out_shape=jax.ShapeDtypeStruct(residual.shape, residual.dtype),
        in_specs=[VMEM, VMEM],
        out_specs=VMEM,
        compiler_params=PARAMS,
        cost_estimate=cost(residual.size, 6 * residual.size),
        name="finish",
    )(owned, residual)


def exchange(value, axes):
    return lax.all_to_all(value, axes, split_axis=0, concat_axis=0, tiled=True)


def turn(value, axis, by):
    return lax.ppermute(value, axis, [(i, (i + by) % G) for i in range(G)])


def gather_ring(value):
    half = value.shape[0] // 2 + FORWARD
    below = turn(value, "zh", 1)
    above = turn(value, "zh", -1)
    return [value, below, above, turn(below[:half], "zh", 1), turn(above[half:], "zh", -1)]


def local(queries, nb_keys, nb_values, nb_lengths, slot_stretch, out_weight, residual):
    per_dev = slot_stretch.shape[1]
    feats = queries.shape[2]
    part = feats // G
    sections = lax.axis_size("segment")
    count = per_dev * G * G
    back = [(i, (i - 1) % sections) for i in range(sections)]
    onward = [(i, (i + 1) % sections) for i in range(sections)]
    x, zh, t = lax.axis_index("x"), lax.axis_index("zh"), lax.axis_index("tp")

    moved = lax.ppermute(queries[0], "segment", back)
    pair = part // HD
    pieces = moved.reshape(per_dev, G, ROWS, G, pair, HD).transpose(1, 3, 0, 4, 2, 5)
    note = jnp.pad(slot_stretch.astype(jnp.bfloat16), ((0, NOTE - 1), (0, HD - per_dev)))
    pieces = jnp.concatenate(
        [
            pieces.reshape(G * G, per_dev * pair * ROWS, HD),
            jnp.broadcast_to(note[None], (G * G,) + note.shape),
        ],
        axis=1,
    )
    spread = exchange(pieces, SEQ)

    own = lax.ppermute(out_weight[0], "segment", back)

    table = spread[:, per_dev * pair * ROWS, :per_dev].astype(jnp.int32).reshape(count)
    ids = jnp.arange(count, dtype=jnp.int32)
    holder, within = ids // per_dev, ids % per_dev
    apart = (holder % G - zh) % G
    rank = jnp.where(apart == 3, 1, jnp.where(apart == 1, 2, jnp.where(apart == 2, 3, 0)))
    place = (rank * G + holder // G) * per_dev + within
    places = jnp.sum(jnp.where(table[None, :] == ids[:, None], place[None, :], 0), axis=1)
    places = lax.ppermute(places, "segment", onward)

    ordered = permute_blocks(spread, table, per_dev)
    picked = exchange(ordered.reshape(G * G, per_dev, pair * ROWS, HD), SEQ)
    picked, places, own = lax.optimization_barrier((picked, places, own))
    picked = picked.reshape(G, G, per_dev, pair, ROWS, HD)

    parts = []
    for chunk in range(CHUNKS):
        answer = attend(picked, nb_keys[0], nb_values[0], nb_lengths[0], chunk, CHUNKS)
        banded = exchange(answer, "x")
        banded, own = lax.optimization_barrier((banded, own))
        weight = [own, turn(own, "x", -1), turn(own, "x", 2), turn(own, "x", 1)]
        parts.append(gather_ring(banded.reshape(-1, feats // CHUNKS)))

    order = (t + jnp.array(AHEAD, dtype=jnp.int32) - x) % G
    partial = project(parts[0], weight, order)
    arrived = []
    for ahead, block in zip(AHEAD, partial):
        moves = []
        for s in range(sections):
            for i in range(G):
                moves.append((s * G + i, (s + 1) % sections * G + (i + ahead) % G))
        arrived.append(lax.ppermute(block, ("segment", "tp"), moves))
    summed = sum_permute(arrived, places)
    owned = exchange(summed.reshape(G * G, per_dev, ROWS, part), SEQ)
    return finish(owned, residual[0])[None]


def solution(mesh):
    sections, _, tp = mesh.devices.shape
    inner = Mesh(mesh.devices.reshape(sections, G, G, tp), ("segment", "x", "zh", "tp"))
    in_specs = (
        P("segment", SEQ, "tp"),
        P("segment", SEQ, None, "tp"),
        P("segment", SEQ, None, "tp"),
        P("segment", SEQ, None),
        P("segment", SEQ),
        P("segment", "tp", SEQ),
        P("segment", SEQ, "tp"),
    )
    out_specs = P("segment", SEQ, "tp")
    return jax.shard_map(local, mesh=inner, in_specs=in_specs, out_specs=out_specs, check_vma=False)
```
